32 devices in a mesh: groups: 2 (over x), expert: 16 (over z, y, core).
Axes of the slice: x: 2, y: 2, z: 4, core: 2. Of those that a mesh axis runs over, the one named last changes fastest.
Arguments:
- tokens: bfloat16 [4096, 2048], P(('groups', 'expert')), parts along dimension 0, may hold values from -6 to 6
- cotangent: bfloat16 [4096, 2048], P(('groups', 'expert')), parts along dimension 0, may hold values from -1.5 to 1.5
- expert_ids: int32 [4096, 3], P(('groups', 'expert')), parts along dimension 0, may hold values from 0 to 15, all different within a row; in each aligned block of 128 rows (0 to 127, 128 to 255, ...) at most 48 rows name the same one
- combine: float32 [4096, 3], P(('groups', 'expert')), parts along dimension 0, may hold values from 0.2 to 1
- w_gate: bfloat16 [16, 2048, 768], P('expert'), may hold values from -0.125 to 0.125
- w_up: bfloat16 [16, 2048, 768], P('expert'), may hold values from -0.125 to 0.125
- w_down: bfloat16 [16, 768, 2048], P('expert'), may hold values from -0.21875 to 0.21875
Outputs:
- mixed: bfloat16 [4096, 2048], P(('groups', 'expert')), parts along dimension 0
- grad_tokens: bfloat16 [4096, 2048], P(('groups', 'expert')), parts along dimension 0
- grad_combine: float32 [4096, 3], P(('groups', 'expert')), parts along dimension 0
The draws below stay inside these ranges and needn't reach their ends.
There are 2 independent parts, one for each index of `groups`. The reference program is written for one: setup_inputs(seed, part) draws one part's arguments, and reference() takes and returns one part's arrays. A program takes and returns all parts, laid end to end along the dimension named above; an argument that names none is the same for every part. Nothing has to cross between parts.
Inputs may be any that keep to these rules, and one draw needn't show every extreme that they name: `expert_ids`: each token names 3 different experts. In the rows of one device (aligned blocks of 128 tokens) no expert is named more than 48 times, a bound that some block reaches.
All inputs are finite; a program needn't handle non-finite values.
Results may differ from the reference program's by a relative error of at most 0.008.
Values may be sent and summed in bfloat16 or wider, within the bound.
A program may use at most 128 MiB of HBM per device.

```python
import math
import jax
import jax.numpy as jnp
import numpy as np
from jax import lax

D = 2048
FF = 768
TOPK = 3
TOK_DEV = 128
EXPERTS = 16
TOKENS = 2048
CAP = 48
N_EXPERT = 16


def level_of(stream_key, extent, pieces, least, top_value):
    level, own = 1.0, jax.random.fold_in(stream_key, 6)
    for axis_at, shards_of in pieces:
        steps = jnp.exp(jax.random.uniform(jax.random.fold_in(own, axis_at), (shards_of,), jnp.float32, least / len(pieces), top_value / len(pieces)))
        level = level * jnp.repeat(steps, extent[axis_at] // shards_of).reshape([-1 if axis == axis_at else 1 for axis in range(len(extent))])
    return level


def shared_out(rng, own, number, rows, number_of, top, limit, slope):
    ranking = jax.random.permutation(rng, number_of)
    heavy_load, usual = portions_of(number_of, rows * top, limit, slope, True), portions_of(number_of, rows * top, limit, slope, False)
    places = jnp.arange(number_of)

    def named(sizes, rotation):
        used = int((sizes > 0).sum())
        fixed = max(1, used // 4)
        passed = fixed + (places - fixed + rotation * (used - fixed)) % max(1, number_of - fixed)
        return jnp.zeros((number_of,), jnp.int32).at[ranking[jnp.where(places < fixed, places, passed)]].set(jnp.asarray(sizes, jnp.int32))

    sizes = jnp.where(number % 4 == 0, named(heavy_load, number // 4), named(usual, number - number // 4 - 1))
    mixed = jax.random.permutation(jax.random.fold_in(own, 3), number_of)
    donor, receiver = mixed[0:number_of // 2 * 2:2], mixed[1:number_of // 2 * 2:2]
    margin = jnp.minimum(sizes[donor] - 1, limit - sizes[receiver]) // 2
    margin = jnp.where((donor == ranking[0]) | (receiver == ranking[0]) | (sizes[receiver] == 0), 0, jnp.maximum(margin, 0))
    passed = jax.random.randint(jax.random.fold_in(own, 4), (number_of // 2,), 0, 1 << 20) % (margin + 1)
    sizes = sizes.at[donor].add(-passed).at[receiver].add(passed)
    items = jnp.searchsorted(jnp.cumsum(sizes), jnp.arange(rows * top), side="right").astype(jnp.int32)
    listing = items.reshape(top, rows).T
    listing = listing[jax.random.permutation(jax.random.fold_in(own, 1), rows)]
    rotation = jax.random.randint(jax.random.fold_in(own, 2), (rows, 1), 0, top)
    return jnp.take_along_axis(listing, (jnp.arange(top)[None, :] + rotation) % top, axis=1)


def portions_of(count, total, limit, lean, full):
    loads = [(1 << 20) // math.isqrt(rank ** lean) + 1 for rank in range(1, count + 1)]
    largest = limit if full else min(limit, max(-(-total // count), total * loads[0] // sum(loads)))
    least = 1 if total - largest >= count - 1 else 0
    given, surplus = [largest] + [least] * (count - 1), total - largest - least * (count - 1)
    while surplus > 0:
        movable = [i for i in range(1, count) if given[i] < largest] or [i for i in range(1, count) if given[i] < limit]
        pool, remaining = sum([loads[i] for i in movable]), surplus
        for i in movable:
            addition = min(limit - given[i], max(1, remaining * loads[i] // pool), surplus)
            given[i] = given[i] + addition
            surplus = surplus - addition
    return np.array(given)


def gaussian(own_key, shape, deviation, bound, cuts=(), held_as=jnp.bfloat16):
    gain = level_of(own_key, shape, cuts, -0.22, 0.18) if cuts else 1.0
    result = jax.random.normal(own_key, shape, jnp.float32) * deviation * gain
    return jnp.minimum(jnp.maximum(result, -bound), bound).astype(held_as)


def setup_inputs(seed: int = 0, part: int = 0) -> dict:
    splits = jax.random.split(jax.random.key(seed), 8)
    own_keys = jax.random.split(jax.random.fold_in(splits[7], part), 8)
    tokens = gaussian(own_keys[0], (TOKENS, D), 1.0, 6.0, ((0, 16),))
    cotangent = gaussian(own_keys[1], (TOKENS, D), 0.25, 1.5, ((0, 16),))
    expert_ids_keys = jax.random.split(jax.random.fold_in(own_keys[2], 1), TOKENS // TOK_DEV)
    expert_ids_turns = jax.random.permutation(jax.random.fold_in(own_keys[2], 3), TOKENS // TOK_DEV)
    expert_ids = jax.vmap(lambda own, number: shared_out(jax.random.fold_in(own_keys[2], 2), own, number, TOK_DEV, EXPERTS, TOPK, CAP, 2))(expert_ids_keys, expert_ids_turns).reshape((TOKENS, TOPK))
    combine = jnp.clip(0.2 + 0.8 * jax.random.uniform(own_keys[3], (TOKENS, TOPK), jnp.float32) ** level_of(own_keys[3], (TOKENS, TOPK), ((0, 16),), -0.2, 0.2), 0.2, 1.0)
    w_gate = gaussian(splits[4], (EXPERTS, D, FF), D ** -0.5, 0.125, ((0, 16),))
    w_up = gaussian(splits[5], (EXPERTS, D, FF), D ** -0.5, 0.125, ((0, 16),))
    w_down = gaussian(splits[6], (EXPERTS, FF, D), FF ** -0.5, 0.21875, ((0, 16),))
    return {"tokens": tokens, "cotangent": cotangent, "expert_ids": expert_ids, "combine": combine, "w_gate": w_gate, "w_up": w_up, "w_down": w_down}


def expert_rows(row_inputs, row_grads, w_gate, w_up, w_down):
    gate = jnp.dot(row_inputs, w_gate, preferred_element_type=jnp.float32)
    upper = jnp.dot(row_inputs, w_up, preferred_element_type=jnp.float32)
    sigmoid_gate = jax.nn.sigmoid(gate)
    activated = gate * sigmoid_gate
    hidden = (activated * upper).astype(jnp.bfloat16)
    output = jnp.dot(hidden, w_down, preferred_element_type=jnp.float32).astype(jnp.bfloat16)
    d_hidden = lax.dot_general(row_grads, w_down, (((1,), (1,)), ((), ())), preferred_element_type=jnp.float32)
    d_gate = (d_hidden * upper * sigmoid_gate * (1.0 + gate * (1.0 - sigmoid_gate))).astype(jnp.bfloat16)
    d_upper = (d_hidden * activated).astype(jnp.bfloat16)
    back_rows = lax.dot_general(d_gate, w_gate, (((1,), (1,)), ((), ())), preferred_element_type=jnp.float32)
    back_rows = back_rows + lax.dot_general(d_upper, w_up, (((1,), (1,)), ((), ())), preferred_element_type=jnp.float32)
    return output, back_rows.astype(jnp.bfloat16)


def reference(tokens, cotangent, expert_ids, combine, w_gate, w_up, w_down):
    row_total = TOKENS * TOPK
    most_rows = N_EXPERT * CAP
    flat_ids = expert_ids.reshape(row_total).astype(jnp.int32)
    sorted_rows = jnp.argsort(flat_ids, stable=True).astype(jnp.int32)
    expert_loads = jnp.sum((flat_ids[:, None] == jnp.arange(EXPERTS, dtype=jnp.int32)[None, :]).astype(jnp.int32), axis=0)
    starts = (jnp.cumsum(expert_loads) - expert_loads).astype(jnp.int32)
    padded_order = jnp.concatenate((sorted_rows, jnp.zeros((most_rows,), jnp.int32)))
    flat_combine = combine.reshape(row_total)

    def one_expert(running, expert):
        mixed_sum, back_sum, grad_sum = running
        picked = lax.dynamic_slice(padded_order, (starts[expert].astype(jnp.int32),), (most_rows,))
        is_valid = jnp.arange(most_rows, dtype=jnp.int32) < expert_loads[expert]
        token_index = picked // TOPK
        row_inputs = tokens[token_index]
        row_grads = cotangent[token_index]
        output, back_rows = expert_rows(row_inputs, row_grads, w_gate[expert], w_up[expert], w_down[expert])
        factor = jnp.where(is_valid, flat_combine[picked], 0.0).astype(jnp.float32)
        out_wide = output.astype(jnp.float32)
        mixed_sum = mixed_sum.at[token_index].add(factor[:, None] * out_wide)
        back_sum = back_sum.at[token_index].add(factor[:, None] * back_rows.astype(jnp.float32))
        dot_terms = jnp.sum(row_grads.astype(jnp.float32) * out_wide, axis=1)
        grad_sum = grad_sum.at[picked].add(jnp.where(is_valid, dot_terms, 0.0).astype(jnp.float32))
        return (mixed_sum, back_sum, grad_sum), None

    start_state = (jnp.zeros((TOKENS, D), jnp.float32), jnp.zeros((TOKENS, D), jnp.float32), jnp.zeros((row_total,), jnp.float32))
    final_state, _ = lax.scan(one_expert, start_state, jnp.arange(EXPERTS, dtype=jnp.int32))
    mixed_sum, back_sum, grad_sum = final_state
    return mixed_sum.astype(jnp.bfloat16), back_sum.astype(jnp.bfloat16), grad_sum.reshape(TOKENS, TOPK)
```

```python
import jax
import jax.numpy as jnp
from jax import lax
from jax.experimental import pallas as pl
from jax.experimental.pallas import tpu as pltpu
from jax.sharding import PartitionSpec as P

PLANE = 4
LAYERS = 4
MESH = pl.DeviceIdType.MESH
ORDER = ((0, 1, 2, 3), (1, 0, 2, 3), (2, 3, 1, 0), (3, 2, 1, 0))
GRAD_STEP = 2


def expert_rows(row_inputs, row_grads, weights):
    w_gate, w_up, w_down = weights
    gate = jnp.dot(row_inputs, w_gate, preferred_element_type=jnp.float32)
    upper = jnp.dot(row_inputs, w_up, preferred_element_type=jnp.float32)
    sigmoid_gate = jax.nn.sigmoid(gate)
    activated = gate * sigmoid_gate
    hidden = (activated * upper).astype(jnp.bfloat16)
    output = jnp.dot(hidden, w_down, preferred_element_type=jnp.float32).astype(jnp.bfloat16)
    d_hidden = lax.dot_general(
        row_grads, w_down, (((1,), (1,)), ((), ())), preferred_element_type=jnp.float32
    )
    d_gate = (d_hidden * upper * sigmoid_gate * (1.0 + gate * (1.0 - sigmoid_gate))).astype(
        jnp.bfloat16
    )
    d_upper = (d_hidden * activated).astype(jnp.bfloat16)
    back_rows = lax.dot_general(
        d_gate, w_gate, (((1,), (1,)), ((), ())), preferred_element_type=jnp.float32
    )
    back_rows = back_rows + lax.dot_general(
        d_upper, w_up, (((1,), (1,)), ((), ())), preferred_element_type=jnp.float32
    )
    return (output, back_rows.astype(jnp.bfloat16))


def on_device(tokens, cotangent, expert_ids, combine, w_gate, w_up, w_down):
    holders = lax.axis_size("expert")
    tok_rows, model_width = tokens.shape
    fanout = expert_ids.shape[1]
    capacity = 2 * tok_rows * fanout // holders
    count_rows = tok_rows * fanout
    flat_ids = expert_ids.reshape(count_rows)
    onehot = (flat_ids[:, None] == jnp.arange(holders, dtype=jnp.int32)[None, :]).astype(jnp.int32)
    rank_in = jnp.sum((jnp.cumsum(onehot, axis=0) - onehot) * onehot, axis=1)
    own_weights = (w_gate[0], w_up[0], w_down[0])
    slot_flat = flat_ids * capacity + rank_in
    total_slots = holders * capacity
    row_of_slot = (
        jnp.full((total_slots,), count_rows, jnp.int32)
        .at[slot_flat]
        .set(jnp.arange(count_rows, dtype=jnp.int32))
    )
    filled = row_of_slot < count_rows
    token_of_slot = jnp.minimum(row_of_slot, count_rows - 1) // fanout
    send_x = jnp.where(filled[:, None], tokens[token_of_slot], 0).reshape(
        holders, capacity, model_width
    )
    send_g = jnp.where(filled[:, None], cotangent[token_of_slot], 0).reshape(
        holders, capacity, model_width
    )
    got_x, got_g = (
        lax.all_to_all(send_x, "expert", split_axis=0, concat_axis=0, tiled=True),
        lax.all_to_all(send_g, "expert", split_axis=0, concat_axis=0, tiled=True),
    )
    flat_out, flat_back = expert_rows(
        got_x.reshape(total_slots, model_width),
        got_g.reshape(total_slots, model_width),
        own_weights,
    )
    result_out = flat_out.reshape(holders, capacity, model_width)
    result_back = flat_back.reshape(holders, capacity, model_width)
    back_out, back_grad = (
        lax.all_to_all(result_out, "expert", split_axis=0, concat_axis=0, tiled=True),
        lax.all_to_all(result_back, "expert", split_axis=0, concat_axis=0, tiled=True),
    )
    out_rows = (
        back_out.reshape(total_slots, model_width)[slot_flat]
        .reshape(tok_rows, fanout, model_width)
        .astype(jnp.float32)
    )
    grad_rows = (
        back_grad.reshape(total_slots, model_width)[slot_flat]
        .reshape(tok_rows, fanout, model_width)
        .astype(jnp.float32)
    )
    mixed = jnp.einsum("tk,tkd->td", combine, out_rows).astype(jnp.bfloat16)
    grad_tokens = jnp.einsum("tk,tkd->td", combine, grad_rows).astype(jnp.bfloat16)
    grad_combine = jnp.einsum("td,tkd->tk", cotangent.astype(jnp.float32), out_rows)
    return (mixed, grad_tokens, grad_combine)


def nt_dot(a, b):
    return lax.dot_general(a, b, (((1,), (1,)), ((), ())), preferred_element_type=jnp.float32)


def fused_kernel(
    x_hbm, g_hbm, ids_ref, comb_ref, wg_hbm, wu_hbm, wd_hbm,
    mixed_ref, grad_ref, gcomb_ref,
    wg, wu, wd, xg, meta, send_rows, recv_rows, gate_buf, up_buf, ret_rows, part, zrecv,
    dsend, drecv,
    w_sem, own_sem, meta_ss, meta_rs, up_ss, down_ss, line_rs, y_ss, y_rs, r_ss, r_rs,
    p_ss, p_rs, d_ss, d_rs,
):
    tok_rows, width = x_hbm.shape
    fanout = ids_ref.shape[0]
    cap = send_rows.shape[3]
    slots = PLANE * cap
    holders = PLANE * LAYERS
    me = lax.axis_index("expert")
    z = me // PLANE
    p = me % PLANE

    def order(t):
        power = 1 + 3 * z + 9 * (z * (z - 1) // 2) + 27 * (z * (z - 1) * (z - 2) // 6)
        code = 0
        for step in range(LAYERS):
            packed = sum(ORDER[layer][step] * 4**layer for layer in range(LAYERS))
            code = code + packed * one_if(t, step)
        return (code // power) % 4

    def one_if(t, step):
        d = (t - step) * (t - step)
        return (10 - d) // 10

    def peer(layer, place):
        return {"expert": layer * PLANE + place}

    def remote(src, dst, ss, rs, dev):
        return pltpu.make_async_remote_copy(
            src_ref=src, dst_ref=dst, send_sem=ss, recv_sem=rs, device_id=dev, device_id_type=MESH
        )

    w_copies = [
        pltpu.make_async_copy(wg_hbm.at[0], wg, w_sem.at[0]),
        pltpu.make_async_copy(wu_hbm.at[0], wu, w_sem.at[1]),
        pltpu.make_async_copy(wd_hbm.at[0], wd, w_sem.at[2]),
    ]
    own_copies = [
        pltpu.make_async_copy(x_hbm, xg.at[0, z], own_sem.at[0]),
        pltpu.make_async_copy(g_hbm, xg.at[1, z], own_sem.at[1]),
    ]
    for copy in own_copies + w_copies:
        copy.start()

    barrier = pltpu.get_barrier_semaphore()
    for o in range(1, LAYERS):
        pl.semaphore_signal(
            barrier, inc=1, device_id=peer((z + o) % LAYERS, p), device_id_type=MESH
        )
    for o in range(1, PLANE):
        pl.semaphore_signal(
            barrier, inc=1, device_id=peer(z, (p + o) % PLANE), device_id_type=MESH
        )

    experts = lax.broadcasted_iota(jnp.int32, (holders, tok_rows), 0)
    chosen = jnp.zeros((holders, tok_rows), jnp.float32)
    weight = jnp.zeros((holders, tok_rows), jnp.float32)
    for k in range(fanout):
        hit = ids_ref[k : k + 1, :] == experts
        chosen = chosen + jnp.where(hit, 1.0, 0.0)
        weight = weight + jnp.where(hit, comb_ref[k : k + 1, :], 0.0)
    earlier = lax.broadcasted_iota(jnp.int32, (tok_rows, tok_rows), 0)
    later = lax.broadcasted_iota(jnp.int32, (tok_rows, tok_rows), 1)
    before = jnp.where(earlier < later, 1.0, 0.0).astype(jnp.bfloat16)
    rank = jnp.dot(chosen.astype(jnp.bfloat16), before, preferred_element_type=jnp.float32)
    rank = jnp.where(chosen > 0.5, rank, -1.0)
    for layer in range(LAYERS):
        at = slice(layer * PLANE, (layer + 1) * PLANE)
        meta[z, layer] = jnp.concatenate([rank[at], weight[at]], axis=0)

    pl.semaphore_wait(barrier, LAYERS + PLANE - 2)

    def meta_copy(o):
        layer = (z + o) % LAYERS
        return remote(
            meta.at[z], meta.at[z], meta_ss.at[layer], meta_rs.at[z], peer(layer, p)
        )

    def meta_wait(s):
        remote(meta.at[s], meta.at[s], meta_ss.at[s], meta_rs.at[s], peer(s, p)).wait_recv()

    def up_copy(ph, s):
        block = xg.at[ph, s]
        return remote(block, block, up_ss.at[ph, s], line_rs.at[ph, s], peer(z + 1, p))

    def down_copy(ph, s):
        block = xg.at[ph, s]
        return remote(block, block, down_ss.at[ph, s], line_rs.at[ph, s], peer(z - 1, p))

    def row_copy(ph, s, q):
        return remote(
            send_rows.at[ph, s, q], recv_rows.at[ph, s, p], y_ss.at[ph, s, q],
            y_rs.at[ph, s, p], peer(z, q),
        )

    def row_wait(ph, s, q):
        remote(
            send_rows.at[ph, s, q], recv_rows.at[ph, s, q], y_ss.at[ph, s, q],
            y_rs.at[ph, s, q], peer(z, q),
        ).wait_recv()

    def ret_copy(ph, s, q):
        return remote(
            recv_rows.at[ph, s, q], ret_rows.at[ph, s, p], r_ss.at[ph, s, q],
            r_rs.at[ph, s, p], peer(z, q),
        )

    def ret_wait(ph, s, q):
        remote(
            recv_rows.at[ph, s, q], ret_rows.at[ph, s, q], r_ss.at[ph, s, q],
            r_rs.at[ph, s, q], peer(z, q),
        ).wait_recv()

    def part_copy(ph, s):
        return remote(
            part.at[ph, s], zrecv.at[ph, z], p_ss.at[ph, s], p_rs.at[ph, z], peer(s, p)
        )

    def dot_copy(s):
        return remote(dsend.at[s], drecv.at[z], d_ss.at[s], d_rs.at[z], peer(s, p))

    def forward(ph, s):
        @pl.when((s <= z) & (z < LAYERS - 1))
        def _():
            up_copy(ph, s).start()

        @pl.when((s >= z) & (z > 0))
        def _():
            down_copy(ph, s).start()

    own_copies[0].wait()
    forward(0, z)
    for o in range(1, LAYERS):
        meta_copy(o).start()
    own_copies[1].wait()
    for copy in w_copies:
        copy.wait()

    row_id = lax.broadcasted_iota(jnp.int32, (cap, tok_rows), 0).astype(jnp.float32)

    def picks(s):
        tables = meta[s, z]
        return [tables[q : q + 1] == row_id for q in range(PLANE)], tables

    def send_stage(i):
        ph, t = i // LAYERS, i % LAYERS
        s = order(t)

        @pl.when(t > 0)
        def _():
            @pl.when(ph == 0)
            def _():
                meta_wait(s)

            remote(
                xg.at[ph, s], xg.at[ph, s], up_ss.at[ph, s], line_rs.at[ph, s], peer(s, p)
            ).wait_recv()
            forward(ph, s)

        @pl.when(i == GRAD_STEP)
        def _():
            forward(1, z)

        hits, _ = picks(s)
        select = jnp.concatenate(
            [jnp.where(hit, 1.0, 0.0) for hit in hits], axis=0
        ).astype(jnp.bfloat16)
        rows = jnp.dot(select, xg[ph, s], preferred_element_type=jnp.float32)
        send_rows[ph, s] = rows.astype(jnp.bfloat16).reshape(PLANE, cap, width)
        for o in range(1, PLANE):
            row_copy(ph, s, (p + o) % PLANE).start()
        recv_rows[ph, s, p] = send_rows[ph, s, p]

    def expert_stage(i):
        ph, t = i // LAYERS, i % LAYERS
        s = order(t)
        for o in range(1, PLANE):
            row_wait(ph, s, (p + o) % PLANE)

        @pl.when(ph == 0)
        def _():
            rows = recv_rows[0, s].reshape(slots, width)
            gate = jnp.dot(rows, wg[...], preferred_element_type=jnp.float32)
            upper = jnp.dot(rows, wu[...], preferred_element_type=jnp.float32)
            gate_buf[s] = gate
            up_buf[s] = upper
            hidden = (gate * jax.nn.sigmoid(gate) * upper).astype(jnp.bfloat16)
            out = jnp.dot(hidden, wd[...], preferred_element_type=jnp.float32)
            recv_rows[0, s] = out.astype(jnp.bfloat16).reshape(PLANE, cap, width)

        @pl.when(ph == 1)
        def _():
            rows = recv_rows[1, s].reshape(slots, width)
            d_hidden = nt_dot(rows, wd[...])
            gate = gate_buf[s]
            upper = up_buf[s]
            sig = jax.nn.sigmoid(gate)
            d_gate = (d_hidden * upper * sig * (1.0 + gate * (1.0 - sig))).astype(jnp.bfloat16)
            d_upper = (d_hidden * (gate * sig)).astype(jnp.bfloat16)
            back = nt_dot(d_gate, wg[...]) + nt_dot(d_upper, wu[...])
            recv_rows[1, s] = back.astype(jnp.bfloat16).reshape(PLANE, cap, width)

        for o in range(1, PLANE):
            ret_copy(ph, s, (p + o) % PLANE).start()
        ret_rows[ph, s, p] = recv_rows[ph, s, p]

    def combine_stage(i):
        ph, t = i // LAYERS, i % LAYERS
        s = order(t)
        for o in range(1, PLANE):
            ret_wait(ph, s, (p + o) % PLANE)
        hits, tables = picks(s)
        weights = jnp.concatenate(
            [
                jnp.where(hits[q], tables[PLANE + q : PLANE + q + 1], 0.0)
                for q in range(PLANE)
            ],
            axis=0,
        )
        high = weights.astype(jnp.bfloat16)
        low = (weights - high.astype(jnp.float32)).astype(jnp.bfloat16)
        rows = ret_rows[ph, s].reshape(slots, width)
        first = (((0,), (0,)), ((), ()))
        total = lax.dot_general(high, rows, first, preferred_element_type=jnp.float32)
        total = total + lax.dot_general(low, rows, first, preferred_element_type=jnp.float32)
        total = total.astype(jnp.bfloat16)

        @pl.when(t == 0)
        def _():
            zrecv[ph, z] = total

        @pl.when(t > 0)
        def _():
            part[ph, s] = total
            part_copy(ph, s).start()

        @pl.when(ph == 1)
        def _():
            out = ret_rows[0, s].reshape(slots, width)
            pairs = nt_dot(out, xg[1, s])
            sums = [
                jnp.sum(
                    jnp.where(hits[q], pairs[q * cap : (q + 1) * cap], 0.0), axis=0, keepdims=True
                )
                for q in range(PLANE)
            ]
            table = jnp.concatenate(sums + [jnp.zeros((8 - PLANE, tok_rows), jnp.float32)], axis=0)

            @pl.when(t == 0)
            def _():
                drecv[z] = table

            @pl.when(t > 0)
            def _():
                dsend[s] = table
                dot_copy(s).start()

    items = 2 * LAYERS

    def step(i, carry):
        @pl.when(i < items)
        def _():
            send_stage(i)

        @pl.when((i >= 1) & (i < items + 1))
        def _():
            expert_stage(i - 1)

        @pl.when(i >= 2)
        def _():
            combine_stage(i - 2)

        return carry

    lax.fori_loop(0, items + 2, step, 0)

    for ph, target in ((0, mixed_ref), (1, grad_ref)):
        for o in range(1, LAYERS):
            s = (z + o) % LAYERS
            remote(
                part.at[ph, s], zrecv.at[ph, s], p_ss.at[ph, s], p_rs.at[ph, s], peer(s, p)
            ).wait_recv()
        total = zrecv[ph, 0].astype(jnp.float32)
        for s in range(1, LAYERS):
            total = total + zrecv[ph, s].astype(jnp.float32)
        target[...] = total.astype(jnp.bfloat16)
    for o in range(1, LAYERS):
        s = (z + o) % LAYERS
        remote(dsend.at[s], drecv.at[s], d_ss.at[s], d_rs.at[s], peer(s, p)).wait_recv()
    table = jnp.concatenate([drecv[layer, :PLANE] for layer in range(LAYERS)], axis=0)
    for k in range(fanout):
        hit = ids_ref[k : k + 1, :] == experts
        gcomb_ref[k : k + 1, :] = jnp.sum(jnp.where(hit, table, 0.0), axis=0, keepdims=True)

    for o in range(1, LAYERS):
        s = (z + o) % LAYERS
        meta_copy(o).wait_send()
        dot_copy(s).wait_send()
        for ph in range(2):
            part_copy(ph, s).wait_send()

    def drain(i, carry):
        ph, s = i // LAYERS, i % LAYERS

        @pl.when((s <= z) & (z < LAYERS - 1))
        def _():
            up_copy(ph, s).wait_send()

        @pl.when((s >= z) & (z > 0))
        def _():
            down_copy(ph, s).wait_send()

        for o in range(1, PLANE):
            row_copy(ph, s, (p + o) % PLANE).wait_send()
            ret_copy(ph, s, (p + o) % PLANE).wait_send()
        return carry

    lax.fori_loop(0, items, drain, 0)


def fused_on_device(tokens, cotangent, expert_ids, combine, w_gate, w_up, w_down):
    holders = lax.axis_size("expert")
    tok_rows, width = tokens.shape
    fanout = expert_ids.shape[1]
    cap = 2 * tok_rows * fanout // holders
    inner = w_gate.shape[2]
    slots = PLANE * cap
    bf, f32 = jnp.bfloat16, jnp.float32
    hbm = pl.BlockSpec(memory_space=pl.ANY)
    vmem = pl.BlockSpec(memory_space=pltpu.VMEM)
    dma = pltpu.SemaphoreType.DMA
    rows = pltpu.VMEM((2, LAYERS, PLANE, cap, width), bf)
    blocks = pltpu.VMEM((2, LAYERS, tok_rows, width), bf)
    mixed, grad_tokens, gcomb = pl.pallas_call(
        fused_kernel,
        out_shape=(
            jax.ShapeDtypeStruct((tok_rows, width), bf),
            jax.ShapeDtypeStruct((tok_rows, width), bf),
            jax.ShapeDtypeStruct((fanout, tok_rows), f32),
        ),
        in_specs=[hbm, hbm, vmem, vmem, hbm, hbm, hbm],
        out_specs=(vmem, vmem, vmem),
        scratch_shapes=[
            pltpu.VMEM(w_gate.shape[1:], bf),
            pltpu.VMEM(w_up.shape[1:], bf),
            pltpu.VMEM(w_down.shape[1:], bf),
            blocks,
            pltpu.VMEM((LAYERS, LAYERS, 2 * PLANE, tok_rows), f32),
            rows,
            rows,
            pltpu.VMEM((LAYERS, slots, inner), f32),
            pltpu.VMEM((LAYERS, slots, inner), f32),
            rows,
            blocks,
            blocks,
            pltpu.VMEM((LAYERS, 8, tok_rows), f32),
            pltpu.VMEM((LAYERS, 8, tok_rows), f32),
            dma((3,)),
            dma((2,)),
            dma((LAYERS,)),
            dma((LAYERS,)),
            dma((2, LAYERS)),
            dma((2, LAYERS)),
            dma((2, LAYERS)),
            dma((2, LAYERS, PLANE)),
            dma((2, LAYERS, PLANE)),
            dma((2, LAYERS, PLANE)),
            dma((2, LAYERS, PLANE)),
            dma((2, LAYERS)),
            dma((2, LAYERS)),
            dma((LAYERS,)),
            dma((LAYERS,)),
        ],
        compiler_params=pltpu.CompilerParams(
            collective_id=0, has_side_effects=True, vmem_limit_bytes=60 * 2**20
        ),
    )(tokens, cotangent, expert_ids.T, combine.T, w_gate, w_up, w_down)
    return mixed, grad_tokens, gcomb.T


def solution(mesh):
    placed = (
        P(("groups", "expert"), None),
        P(("groups", "expert"), None),
        P(("groups", "expert"), None),
        P(("groups", "expert"), None),
        P("expert", None, None),
        P("expert", None, None),
        P("expert", None, None),
    )
    fits = mesh.shape["expert"] == PLANE * LAYERS
    return jax.shard_map(
        fused_on_device if fits else on_device,
        mesh=mesh,
        in_specs=placed,
        out_specs=(
            P(("groups", "expert"), None),
            P(("groups", "expert"), None),
            P(("groups", "expert"), None),
        ),
        check_vma=False,
    )
```

```python
import functools

import jax
import jax.numpy as jnp
from jax import lax
from jax.experimental import pallas as pl
from jax.experimental.pallas import tpu as pltpu
from jax.sharding import PartitionSpec as P

PLANE = 4
LAYERS = 4
MESH = pl.DeviceIdType.MESH
CHAINED = 1
SCHEDULE = (
    ("line", 0),
    ("grad", 4),
    ("send", 0),
    ("weight", 1),
    ("expert", 1),
    ("combine", 2),
    ("relay", 3),
    ("chain", 5),
)
ORDER = ((0, 1, 2, 3), (1, 0, 2, 3), (2, 3, 1, 0), (3, 2, 1, 0))


def expert_rows(row_inputs, row_grads, weights):
    w_gate, w_up, w_down = weights
    gate = jnp.dot(row_inputs, w_gate, preferred_element_type=jnp.float32)
    upper = jnp.dot(row_inputs, w_up, preferred_element_type=jnp.float32)
    sigmoid_gate = jax.nn.sigmoid(gate)
    activated = gate * sigmoid_gate
    hidden = (activated * upper).astype(jnp.bfloat16)
    output = jnp.dot(hidden, w_down, preferred_element_type=jnp.float32).astype(jnp.bfloat16)
    d_hidden = lax.dot_general(
        row_grads, w_down, (((1,), (1,)), ((), ())), preferred_element_type=jnp.float32
    )
    d_gate = (d_hidden * upper * sigmoid_gate * (1.0 + gate * (1.0 - sigmoid_gate))).astype(
        jnp.bfloat16
    )
    d_upper = (d_hidden * activated).astype(jnp.bfloat16)
    back_rows = lax.dot_general(
        d_gate, w_gate, (((1,), (1,)), ((), ())), preferred_element_type=jnp.float32
    )
    back_rows = back_rows + lax.dot_general(
        d_upper, w_up, (((1,), (1,)), ((), ())), preferred_element_type=jnp.float32
    )
    return (output, back_rows.astype(jnp.bfloat16))


def on_device(tokens, cotangent, expert_ids, combine, w_gate, w_up, w_down):
    holders = lax.axis_size("expert")
    tok_rows, model_width = tokens.shape
    fanout = expert_ids.shape[1]
    capacity = 2 * tok_rows * fanout // holders
    count_rows = tok_rows * fanout
    flat_ids = expert_ids.reshape(count_rows)
    onehot = (flat_ids[:, None] == jnp.arange(holders, dtype=jnp.int32)[None, :]).astype(jnp.int32)
    rank_in = jnp.sum((jnp.cumsum(onehot, axis=0) - onehot) * onehot, axis=1)
    own_weights = (w_gate[0], w_up[0], w_down[0])
    slot_flat = flat_ids * capacity + rank_in
    total_slots = holders * capacity
    row_of_slot = (
        jnp.full((total_slots,), count_rows, jnp.int32)
        .at[slot_flat]
        .set(jnp.arange(count_rows, dtype=jnp.int32))
    )
    filled = row_of_slot < count_rows
    token_of_slot = jnp.minimum(row_of_slot, count_rows - 1) // fanout
    send_x = jnp.where(filled[:, None], tokens[token_of_slot], 0).reshape(
        holders, capacity, model_width
    )
    send_g = jnp.where(filled[:, None], cotangent[token_of_slot], 0).reshape(
        holders, capacity, model_width
    )
    got_x, got_g = (
        lax.all_to_all(send_x, "expert", split_axis=0, concat_axis=0, tiled=True),
        lax.all_to_all(send_g, "expert", split_axis=0, concat_axis=0, tiled=True),
    )
    flat_out, flat_back = expert_rows(
        got_x.reshape(total_slots, model_width),
        got_g.reshape(total_slots, model_width),
        own_weights,
    )
    result_out = flat_out.reshape(holders, capacity, model_width)
    result_back = flat_back.reshape(holders, capacity, model_width)
    back_out, back_grad = (
        lax.all_to_all(result_out, "expert", split_axis=0, concat_axis=0, tiled=True),
        lax.all_to_all(result_back, "expert", split_axis=0, concat_axis=0, tiled=True),
    )
    out_rows = (
        back_out.reshape(total_slots, model_width)[slot_flat]
        .reshape(tok_rows, fanout, model_width)
        .astype(jnp.float32)
    )
    grad_rows = (
        back_grad.reshape(total_slots, model_width)[slot_flat]
        .reshape(tok_rows, fanout, model_width)
        .astype(jnp.float32)
    )
    mixed = jnp.einsum("tk,tkd->td", combine, out_rows).astype(jnp.bfloat16)
    grad_tokens = jnp.einsum("tk,tkd->td", combine, grad_rows).astype(jnp.bfloat16)
    grad_combine = jnp.einsum("td,tkd->tk", cotangent.astype(jnp.float32), out_rows)
    return (mixed, grad_tokens, grad_combine)


def nt_dot(a, b):
    return lax.dot_general(a, b, (((1,), (1,)), ((), ())), preferred_element_type=jnp.float32)


def fused_kernel(
    x_hbm, g_hbm, ids_ref, comb_ref, wg_hbm, wu_hbm, wd_hbm,
    mixed_ref, grad_ref, gcomb_ref,
    wg, wu, wd, xg, meta, send_rows, recv_rows, gate_buf, up_buf, ret_rows, part, zrecv, relay, chain,
    dsend, drecv,
    w_sem, own_sem, meta_ss, meta_rs, up_ss, down_ss, line_rs, y_ss, y_rs, r_ss, r_rs,
    p_ss, p_rs, d_ss, d_rs, relay_rs, chain_rs,
):
    tok_rows, width = x_hbm.shape
    fanout = ids_ref.shape[0]
    cap = send_rows.shape[3]
    slots = PLANE * cap
    holders = PLANE * LAYERS
    me = lax.axis_index("expert")
    z = me // PLANE
    p = me % PLANE

    def order(t):
        power = 1 + 3 * z + 9 * (z * (z - 1) // 2) + 27 * (z * (z - 1) * (z - 2) // 6)
        code = 0
        for step in range(LAYERS):
            packed = sum(ORDER[layer][step] * 4**layer for layer in range(LAYERS))
            code = code + packed * one_if(t, step)
        return (code // power) % 4

    def item(i):
        first = (i // 2 + 2) // 3
        return (1 - first) * i + first * ((i + 1) // 6), first * ((i + 1) % 3 + 1)

    def one_if(t, step):
        d = (t - step) * (t - step)
        return (10 - d) // 10

    def peer(layer, place):
        return {"expert": layer * PLANE + place}

    def remote(src, dst, ss, rs, dev):
        return pltpu.make_async_remote_copy(
            src_ref=src, dst_ref=dst, send_sem=ss, recv_sem=rs, device_id=dev, device_id_type=MESH
        )

    w_copies = [
        pltpu.make_async_copy(wg_hbm.at[0], wg, w_sem.at[0]),
        pltpu.make_async_copy(wu_hbm.at[0], wu, w_sem.at[1]),
        pltpu.make_async_copy(wd_hbm.at[0], wd, w_sem.at[2]),
    ]
    own_copies = [
        pltpu.make_async_copy(x_hbm, xg.at[0, z], own_sem.at[0]),
        pltpu.make_async_copy(g_hbm, xg.at[1, z], own_sem.at[1]),
    ]
    for copy in own_copies + w_copies:
        copy.start()

    barrier = pltpu.get_barrier_semaphore()
    for o in range(1, LAYERS):
        pl.semaphore_signal(
            barrier, inc=1, device_id=peer((z + o) % LAYERS, p), device_id_type=MESH
        )
    for o in range(1, PLANE):
        pl.semaphore_signal(
            barrier, inc=1, device_id=peer(z, (p + o) % PLANE), device_id_type=MESH
        )

    experts = lax.broadcasted_iota(jnp.int32, (holders, tok_rows), 0)
    chosen = jnp.zeros((holders, tok_rows), jnp.float32)
    weight = jnp.zeros((holders, tok_rows), jnp.float32)
    for k in range(fanout):
        hit = ids_ref[k : k + 1, :] == experts
        chosen = chosen + jnp.where(hit, 1.0, 0.0)
        weight = weight + jnp.where(hit, comb_ref[k : k + 1, :], 0.0)
    earlier = lax.broadcasted_iota(jnp.int32, (tok_rows, tok_rows), 0)
    later = lax.broadcasted_iota(jnp.int32, (tok_rows, tok_rows), 1)
    before = jnp.where(earlier < later, 1.0, 0.0).astype(jnp.bfloat16)
    rank = jnp.dot(chosen.astype(jnp.bfloat16), before, preferred_element_type=jnp.float32)
    rank = jnp.where(chosen > 0.5, rank, -1.0)
    for layer in range(LAYERS):
        at = slice(layer * PLANE, (layer + 1) * PLANE)
        meta[z, layer] = jnp.concatenate([rank[at], weight[at]], axis=0)

    pl.semaphore_wait(barrier, LAYERS + PLANE - 2)

    def meta_copy(o):
        layer = (z + o) % LAYERS
        return remote(
            meta.at[z], meta.at[z], meta_ss.at[layer], meta_rs.at[z], peer(layer, p)
        )

    def meta_wait(s):
        remote(meta.at[s], meta.at[s], meta_ss.at[s], meta_rs.at[s], peer(s, p)).wait_recv()

    def up_copy(ph, s):
        block = xg.at[ph, s]
        return remote(block, block, up_ss.at[ph, s], line_rs.at[ph, s], peer(z + 1, p))

    def down_copy(ph, s):
        block = xg.at[ph, s]
        return remote(block, block, down_ss.at[ph, s], line_rs.at[ph, s], peer(z - 1, p))

    def row_copy(ph, s, q):
        return remote(
            send_rows.at[ph, s, q], recv_rows.at[ph, s, p], y_ss.at[ph, s, q],
            y_rs.at[ph, s, p], peer(z, q),
        )

    def row_wait(ph, s, q):
        remote(
            send_rows.at[ph, s, q], recv_rows.at[ph, s, q], y_ss.at[ph, s, q],
            y_rs.at[ph, s, q], peer(z, q),
        ).wait_recv()

    def ret_copy(ph, s, q):
        return remote(
            recv_rows.at[ph, s, q], ret_rows.at[ph, s, p], r_ss.at[ph, s, q],
            r_rs.at[ph, s, p], peer(z, q),
        )

    def ret_wait(ph, s, q):
        remote(
            recv_rows.at[ph, s, q], ret_rows.at[ph, s, q], r_ss.at[ph, s, q],
            r_rs.at[ph, s, q], peer(z, q),
        ).wait_recv()

    mate = z + 1 - 2 * (z % 2)
    inner = (z >= 1) & (z <= LAYERS - 2)
    outer = (z < 1) | (z > LAYERS - 2)
    other_inner = 2 - z // 2

    def part_copy(ph, s):
        return remote(
            part.at[ph, s], zrecv.at[ph, z], p_ss.at[ph, s], p_rs.at[ph, z], peer(s, p)
        )

    def part_wait(ph, s):
        remote(
            part.at[ph, s], zrecv.at[ph, s], p_ss.at[ph, s], p_rs.at[ph, s], peer(s, p)
        ).wait_recv()

    def chain_copy(ph, s):
        return remote(
            part.at[ph, s], chain.at[ph], p_ss.at[ph, s], chain_rs.at[ph], peer(other_inner, p)
        )

    def relay_copy(ph, s):
        return remote(
            part.at[ph, s], relay.at[ph, s % 2], p_ss.at[ph, s], relay_rs.at[ph, s % 2],
            peer(mate, p),
        )

    def dot_copy(s):
        return remote(dsend.at[s], drecv.at[z], d_ss.at[s], d_rs.at[z], peer(s, p))

    def forward(ph, s):
        @pl.when((s <= z) & (z < LAYERS - 1))
        def _():
            up_copy(ph, s).start()

        @pl.when((s >= z) & (z > 0))
        def _():
            down_copy(ph, s).start()

    own_copies[0].wait()
    forward(0, z)
    for o in range(1, LAYERS):
        meta_copy(o).start()
    own_copies[1].wait()

    row_id = lax.broadcasted_iota(jnp.int32, (cap, tok_rows), 0).astype(jnp.float32)

    def picks(s):
        tables = meta[s, z]
        return [tables[q : q + 1] == row_id for q in range(PLANE)], tables

    def line_stage(i):
        ph, t = item(i)
        s = order(t)

        @pl.when(t > 0)
        def _():
            @pl.when(ph == 0)
            def _():
                meta_wait(s)

            remote(
                xg.at[ph, s], xg.at[ph, s], up_ss.at[ph, s], line_rs.at[ph, s], peer(s, p)
            ).wait_recv()
            forward(ph, s)

    def send_stage(i):
        ph, t = item(i)
        s = order(t)

        hits, _ = picks(s)
        select = jnp.concatenate(
            [jnp.where(hit, 1.0, 0.0) for hit in hits], axis=0
        ).astype(jnp.bfloat16)
        rows = jnp.dot(select, xg[ph, s], preferred_element_type=jnp.float32)
        send_rows[ph, s] = rows.astype(jnp.bfloat16).reshape(PLANE, cap, width)
        for o in range(1, PLANE):
            row_copy(ph, s, (p + o) % PLANE).start()
        recv_rows[ph, s, p] = send_rows[ph, s, p]

    def expert_stage(i):
        ph, t = item(i)
        s = order(t)
        for o in range(1, PLANE):
            row_wait(ph, s, (p + o) % PLANE)

        @pl.when(ph == 0)
        def _():
            rows = recv_rows[0, s].reshape(slots, width)
            gate = jnp.dot(rows, wg[...], preferred_element_type=jnp.float32)
            upper = jnp.dot(rows, wu[...], preferred_element_type=jnp.float32)
            gate_buf[s] = gate
            up_buf[s] = upper
            hidden = (gate * jax.nn.sigmoid(gate) * upper).astype(jnp.bfloat16)
            out = jnp.dot(hidden, wd[...], preferred_element_type=jnp.float32)
            recv_rows[0, s] = out.astype(jnp.bfloat16).reshape(PLANE, cap, width)

        @pl.when(ph == 1)
        def _():
            rows = recv_rows[1, s].reshape(slots, width)
            d_hidden = nt_dot(rows, wd[...])
            gate = gate_buf[s]
            upper = up_buf[s]
            sig = jax.nn.sigmoid(gate)
            d_gate = (d_hidden * upper * sig * (1.0 + gate * (1.0 - sig))).astype(jnp.bfloat16)
            d_upper = (d_hidden * (gate * sig)).astype(jnp.bfloat16)
            back = nt_dot(d_gate, wg[...]) + nt_dot(d_upper, wu[...])
            recv_rows[1, s] = back.astype(jnp.bfloat16).reshape(PLANE, cap, width)

        for o in range(1, PLANE):
            ret_copy(ph, s, (p + o) % PLANE).start()
        ret_rows[ph, s, p] = recv_rows[ph, s, p]

    def combine_stage(i):
        ph, t = item(i)
        s = order(t)
        for o in range(1, PLANE):
            ret_wait(ph, s, (p + o) % PLANE)
        hits, tables = picks(s)
        weights = jnp.concatenate(
            [
                jnp.where(hits[q], tables[PLANE + q : PLANE + q + 1], 0.0)
                for q in range(PLANE)
            ],
            axis=0,
        )
        high = weights.astype(jnp.bfloat16)
        low = (weights - high.astype(jnp.float32)).astype(jnp.bfloat16)
        rows = ret_rows[ph, s].reshape(slots, width)
        first = (((0,), (0,)), ((), ()))
        total = lax.dot_general(high, rows, first, preferred_element_type=jnp.float32)
        total = total + lax.dot_general(low, rows, first, preferred_element_type=jnp.float32)
        total = total.astype(jnp.bfloat16)

        @pl.when(t == 0)
        def _():
            zrecv[ph, z] = total

        @pl.when(t > 0)
        def _():
            part[ph, s] = total

        @pl.when((t == 1) & (outer | (ph >= CHAINED)))
        def _():
            part_copy(ph, s).start()

        @pl.when((t > 1) & outer)
        def _():
            relay_copy(ph, s).start()

        @pl.when(ph == 1)
        def _():
            out = ret_rows[0, s].reshape(slots, width)
            pairs = nt_dot(out, xg[1, s])
            sums = [
                jnp.sum(
                    jnp.where(hits[q], pairs[q * cap : (q + 1) * cap], 0.0), axis=0, keepdims=True
                )
                for q in range(PLANE)
            ]
            table = jnp.concatenate(sums + [jnp.zeros((8 - PLANE, tok_rows), jnp.float32)], axis=0)

            @pl.when(t == 0)
            def _():
                drecv[z] = table

            @pl.when(t > 0)
            def _():
                dsend[s] = table
                dot_copy(s).start()

    def relay_stage(i):
        ph, t = item(i)
        s = order(t)

        @pl.when((t > 1) & inner)
        def _():
            relay_copy(ph, s).wait_recv()
            total = part[ph, s].astype(jnp.float32) + relay[ph, s % 2].astype(jnp.float32)
            part[ph, s] = total.astype(jnp.bfloat16)

            @pl.when((t < LAYERS - 1) | (ph >= CHAINED))
            def _():
                part_copy(ph, s).start()

            @pl.when((t == LAYERS - 1) & (ph < CHAINED))
            def _():
                chain_copy(ph, s).start()

    def chain_stage(i):
        ph, t = item(i)

        @pl.when((t == LAYERS - 1) & (ph < CHAINED) & inner)
        def _():
            chain_copy(ph, mate).wait_recv()
            total = part[ph, mate].astype(jnp.float32) + chain[ph].astype(jnp.float32)
            part[ph, mate] = total.astype(jnp.bfloat16)
            part_copy(ph, mate).start()

    items = 2 * LAYERS

    def grad_stage(i):
        @pl.when(i == 0)
        def _():
            forward(1, z)

    def weight_stage(i):
        @pl.when(i == 0)
        def _():
            for copy in w_copies:
                copy.wait()

    stages = {
        "line": line_stage,
        "grad": grad_stage,
        "send": send_stage,
        "weight": weight_stage,
        "expert": expert_stage,
        "combine": combine_stage,
        "relay": relay_stage,
        "chain": chain_stage,
    }
    last = items + max(lag for _, lag in SCHEDULE)

    def step(i, carry):
        for name, lag in SCHEDULE:
            pl.when((i >= lag) & (i < items + lag))(functools.partial(stages[name], i - lag))
        return carry

    lax.fori_loop(0, last, step, 0)

    for ph, target in ((0, mixed_ref), (1, grad_ref)):
        part_wait(ph, mate)
        total = zrecv[ph, z].astype(jnp.float32) + zrecv[ph, mate].astype(jnp.float32)

        def add_other(target=target, ph=ph, total=total):
            part_wait(ph, other_inner)
            wide = total + zrecv[ph, other_inner].astype(jnp.float32)
            target[...] = wide.astype(jnp.bfloat16)

        if ph < CHAINED:

            @pl.when(outer)
            def _():
                target[...] = total.astype(jnp.bfloat16)

            pl.when(inner)(add_other)
        else:
            add_other()
    for o in range(1, LAYERS):
        s = (z + o) % LAYERS
        remote(dsend.at[s], drecv.at[s], d_ss.at[s], d_rs.at[s], peer(s, p)).wait_recv()
    table = jnp.concatenate([drecv[layer, :PLANE] for layer in range(LAYERS)], axis=0)
    for k in range(fanout):
        hit = ids_ref[k : k + 1, :] == experts
        gcomb_ref[k : k + 1, :] = jnp.sum(jnp.where(hit, table, 0.0), axis=0, keepdims=True)

    for o in range(1, LAYERS):
        s = (z + o) % LAYERS
        meta_copy(o).wait_send()
        dot_copy(s).wait_send()
        for ph in range(2):
            part_copy(ph, s).wait_send()

    def drain(i, carry):
        ph, s = i // LAYERS, i % LAYERS

        @pl.when((s <= z) & (z < LAYERS - 1))
        def _():
            up_copy(ph, s).wait_send()

        @pl.when((s >= z) & (z > 0))
        def _():
            down_copy(ph, s).wait_send()

        for o in range(1, PLANE):
            row_copy(ph, s, (p + o) % PLANE).wait_send()
            ret_copy(ph, s, (p + o) % PLANE).wait_send()
        return carry

    lax.fori_loop(0, items, drain, 0)


def fused_on_device(tokens, cotangent, expert_ids, combine, w_gate, w_up, w_down):
    holders = lax.axis_size("expert")
    tok_rows, width = tokens.shape
    fanout = expert_ids.shape[1]
    cap = 2 * tok_rows * fanout // holders
    inner = w_gate.shape[2]
    slots = PLANE * cap
    bf, f32 = jnp.bfloat16, jnp.float32
    hbm = pl.BlockSpec(memory_space=pl.ANY)
    vmem = pl.BlockSpec(memory_space=pltpu.VMEM)
    dma = pltpu.SemaphoreType.DMA
    rows = pltpu.VMEM((2, LAYERS, PLANE, cap, width), bf)
    blocks = pltpu.VMEM((2, LAYERS, tok_rows, width), bf)
    mixed, grad_tokens, gcomb = pl.pallas_call(
        fused_kernel,
        out_shape=(
            jax.ShapeDtypeStruct((tok_rows, width), bf),
            jax.ShapeDtypeStruct((tok_rows, width), bf),
            jax.ShapeDtypeStruct((fanout, tok_rows), f32),
        ),
        in_specs=[hbm, hbm, vmem, vmem, hbm, hbm, hbm],
        out_specs=(vmem, vmem, vmem),
        scratch_shapes=[
            pltpu.VMEM(w_gate.shape[1:], bf),
            pltpu.VMEM(w_up.shape[1:], bf),
            pltpu.VMEM(w_down.shape[1:], bf),
            blocks,
            pltpu.VMEM((LAYERS, LAYERS, 2 * PLANE, tok_rows), f32),
            rows,
            rows,
            pltpu.VMEM((LAYERS, slots, inner), f32),
            pltpu.VMEM((LAYERS, slots, inner), f32),
            rows,
            blocks,
            blocks,
            pltpu.VMEM((2, 2, tok_rows, width), bf),
            pltpu.VMEM((2, tok_rows, width), bf),
            pltpu.VMEM((LAYERS, 8, tok_rows), f32),
            pltpu.VMEM((LAYERS, 8, tok_rows), f32),
            dma((3,)),
            dma((2,)),
            dma((LAYERS,)),
            dma((LAYERS,)),
            dma((2, LAYERS)),
            dma((2, LAYERS)),
            dma((2, LAYERS)),
            dma((2, LAYERS, PLANE)),
            dma((2, LAYERS, PLANE)),
            dma((2, LAYERS, PLANE)),
            dma((2, LAYERS, PLANE)),
            dma((2, LAYERS)),
            dma((2, LAYERS)),
            dma((LAYERS,)),
            dma((LAYERS,)),
            dma((2, 2)),
            dma((2,)),
        ],
        compiler_params=pltpu.CompilerParams(
            collective_id=0, has_side_effects=True, vmem_limit_bytes=60 * 2**20
        ),
    )(tokens, cotangent, expert_ids.T, combine.T, w_gate, w_up, w_down)
    return mixed, grad_tokens, gcomb.T


def solution(mesh):
    placed = (
        P(("groups", "expert"), None),
        P(("groups", "expert"), None),
        P(("groups", "expert"), None),
        P(("groups", "expert"), None),
        P("expert", None, None),
        P("expert", None, None),
        P("expert", None, None),
    )
    fits = mesh.shape["expert"] == PLANE * LAYERS
    return jax.shard_map(
        fused_on_device if fits else on_device,
        mesh=mesh,
        in_specs=placed,
        out_specs=(
            P(("groups", "expert"), None),
            P(("groups", "expert"), None),
            P(("groups", "expert"), None),
        ),
        check_vma=False,
    )
```

```python
import functools

import jax
import jax.numpy as jnp
from jax import lax
from jax.experimental import pallas as pl
from jax.experimental.pallas import tpu as pltpu
from jax.sharding import PartitionSpec as P

PLANE = 4
LAYERS = 4
MESH = pl.DeviceIdType.MESH
CHAINED = 1
SCHEDULE = (
    ("line", 0),
    ("grad", 4),
    ("send", 0),
    ("weight", 1),
    ("expert", 1),
    ("combine", 2),
    ("relay", 3),
    ("chain", 5),
)
ORDER = ((0, 1, 2, 3), (1, 0, 2, 3), (2, 3, 1, 0), (3, 2, 1, 0))


def expert_rows(row_inputs, row_grads, weights):
    w_gate, w_up, w_down = weights
    gate = jnp.dot(row_inputs, w_gate, preferred_element_type=jnp.float32)
    upper = jnp.dot(row_inputs, w_up, preferred_element_type=jnp.float32)
    sigmoid_gate = jax.nn.sigmoid(gate)
    activated = gate * sigmoid_gate
    hidden = (activated * upper).astype(jnp.bfloat16)
    output = jnp.dot(hidden, w_down, preferred_element_type=jnp.float32).astype(jnp.bfloat16)
    d_hidden = lax.dot_general(
        row_grads, w_down, (((1,), (1,)), ((), ())), preferred_element_type=jnp.float32
    )
    d_gate = (d_hidden * upper * sigmoid_gate * (1.0 + gate * (1.0 - sigmoid_gate))).astype(
        jnp.bfloat16
    )
    d_upper = (d_hidden * activated).astype(jnp.bfloat16)
    back_rows = lax.dot_general(
        d_gate, w_gate, (((1,), (1,)), ((), ())), preferred_element_type=jnp.float32
    )
    back_rows = back_rows + lax.dot_general(
        d_upper, w_up, (((1,), (1,)), ((), ())), preferred_element_type=jnp.float32
    )
    return (output, back_rows.astype(jnp.bfloat16))


def on_device(tokens, cotangent, expert_ids, combine, w_gate, w_up, w_down):
    holders = lax.axis_size("expert")
    tok_rows, model_width = tokens.shape
    fanout = expert_ids.shape[1]
    capacity = 2 * tok_rows * fanout // holders
    count_rows = tok_rows * fanout
    flat_ids = expert_ids.reshape(count_rows)
    onehot = (flat_ids[:, None] == jnp.arange(holders, dtype=jnp.int32)[None, :]).astype(jnp.int32)
    rank_in = jnp.sum((jnp.cumsum(onehot, axis=0) - onehot) * onehot, axis=1)
    own_weights = (w_gate[0], w_up[0], w_down[0])
    slot_flat = flat_ids * capacity + rank_in
    total_slots = holders * capacity
    row_of_slot = (
        jnp.full((total_slots,), count_rows, jnp.int32)
        .at[slot_flat]
        .set(jnp.arange(count_rows, dtype=jnp.int32))
    )
    filled = row_of_slot < count_rows
    token_of_slot = jnp.minimum(row_of_slot, count_rows - 1) // fanout
    send_x = jnp.where(filled[:, None], tokens[token_of_slot], 0).reshape(
        holders, capacity, model_width
    )
    send_g = jnp.where(filled[:, None], cotangent[token_of_slot], 0).reshape(
        holders, capacity, model_width
    )
    got_x, got_g = (
        lax.all_to_all(send_x, "expert", split_axis=0, concat_axis=0, tiled=True),
        lax.all_to_all(send_g, "expert", split_axis=0, concat_axis=0, tiled=True),
    )
    flat_out, flat_back = expert_rows(
        got_x.reshape(total_slots, model_width),
        got_g.reshape(total_slots, model_width),
        own_weights,
    )
    result_out = flat_out.reshape(holders, capacity, model_width)
    result_back = flat_back.reshape(holders, capacity, model_width)
    back_out, back_grad = (
        lax.all_to_all(result_out, "expert", split_axis=0, concat_axis=0, tiled=True),
        lax.all_to_all(result_back, "expert", split_axis=0, concat_axis=0, tiled=True),
    )
    out_rows = (
        back_out.reshape(total_slots, model_width)[slot_flat]
        .reshape(tok_rows, fanout, model_width)
        .astype(jnp.float32)
    )
    grad_rows = (
        back_grad.reshape(total_slots, model_width)[slot_flat]
        .reshape(tok_rows, fanout, model_width)
        .astype(jnp.float32)
    )
    mixed = jnp.einsum("tk,tkd->td", combine, out_rows).astype(jnp.bfloat16)
    grad_tokens = jnp.einsum("tk,tkd->td", combine, grad_rows).astype(jnp.bfloat16)
    grad_combine = jnp.einsum("td,tkd->tk", cotangent.astype(jnp.float32), out_rows)
    return (mixed, grad_tokens, grad_combine)


def nt_dot(a, b):
    return lax.dot_general(a, b, (((1,), (1,)), ((), ())), preferred_element_type=jnp.float32)


def fused_kernel(
    x_hbm, g_hbm, ids_ref, comb_ref, wg_hbm, wu_hbm, wd_hbm,
    mixed_ref, grad_ref, gcomb_ref,
    wg, wu, wd, xg, meta, send_rows, recv_rows, gate_buf, up_buf, ret_rows, part, zrecv, relay, chain,
    dsend, drecv,
    w_sem, own_sem, meta_ss, meta_rs, up_ss, down_ss, line_rs, y_ss, y_rs, r_ss, r_rs,
    p_ss, p_rs, d_ss, d_rs, relay_rs, chain_rs,
):
    tok_rows, width = x_hbm.shape
    fanout = ids_ref.shape[0]
    cap = send_rows.shape[3]
    slots = PLANE * cap
    holders = PLANE * LAYERS
    me = lax.axis_index("expert")
    z = me // PLANE
    p = me % PLANE

    def order(t):
        power = 1 + 3 * z + 9 * (z * (z - 1) // 2) + 27 * (z * (z - 1) * (z - 2) // 6)
        code = 0
        for step in range(LAYERS):
            packed = sum(ORDER[layer][step] * 4**layer for layer in range(LAYERS))
            code = code + packed * one_if(t, step)
        return (code // power) % 4

    def item(i):
        first = (i // 2 + 2) // 3
        return (1 - first) * i + first * ((i + 1) // 6), first * ((i + 1) % 3 + 1)

    def one_if(t, step):
        d = (t - step) * (t - step)
        return (10 - d) // 10

    def peer(layer, place):
        return {"expert": layer * PLANE + place}

    def remote(src, dst, ss, rs, dev):
        return pltpu.make_async_remote_copy(
            src_ref=src, dst_ref=dst, send_sem=ss, recv_sem=rs, device_id=dev, device_id_type=MESH
        )

    w_copies = [
        pltpu.make_async_copy(wg_hbm.at[0], wg, w_sem.at[0]),
        pltpu.make_async_copy(wu_hbm.at[0], wu, w_sem.at[1]),
        pltpu.make_async_copy(wd_hbm.at[0], wd, w_sem.at[2]),
    ]
    own_copies = [
        pltpu.make_async_copy(x_hbm, xg.at[0, z], own_sem.at[0]),
        pltpu.make_async_copy(g_hbm, xg.at[1, z], own_sem.at[1]),
    ]
    for copy in own_copies:
        copy.start()

    barrier = pltpu.get_barrier_semaphore()
    for o in range(1, LAYERS):
        pl.semaphore_signal(
            barrier, inc=1, device_id=peer((z + o) % LAYERS, p), device_id_type=MESH
        )
    for o in range(1, PLANE):
        pl.semaphore_signal(
            barrier, inc=1, device_id=peer(z, (p + o) % PLANE), device_id_type=MESH
        )

    experts = lax.broadcasted_iota(jnp.int32, (holders, tok_rows), 0)
    chosen = jnp.zeros((holders, tok_rows), jnp.float32)
    weight = jnp.zeros((holders, tok_rows), jnp.float32)
    for k in range(fanout):
        hit = ids_ref[k : k + 1, :] == experts
        chosen = chosen + jnp.where(hit, 1.0, 0.0)
        weight = weight + jnp.where(hit, comb_ref[k : k + 1, :], 0.0)
    earlier = lax.broadcasted_iota(jnp.int32, (tok_rows, tok_rows), 0)
    later = lax.broadcasted_iota(jnp.int32, (tok_rows, tok_rows), 1)
    before = jnp.where(earlier < later, 1.0, 0.0).astype(jnp.bfloat16)
    rank = jnp.dot(chosen.astype(jnp.bfloat16), before, preferred_element_type=jnp.float32)
    rank = jnp.where(chosen > 0.5, rank, -1.0)
    for layer in range(LAYERS):
        at = slice(layer * PLANE, (layer + 1) * PLANE)
        meta[z, layer] = jnp.concatenate([rank[at], weight[at]], axis=0)

    pl.semaphore_wait(barrier, LAYERS + PLANE - 2)

    def meta_copy(o):
        layer = (z + o) % LAYERS
        return remote(
            meta.at[z], meta.at[z], meta_ss.at[layer], meta_rs.at[z], peer(layer, p)
        )

    def meta_wait(s):
        remote(meta.at[s], meta.at[s], meta_ss.at[s], meta_rs.at[s], peer(s, p)).wait_recv()

    def up_copy(ph, s):
        block = xg.at[ph, s]
        return remote(block, block, up_ss.at[ph, s], line_rs.at[ph, s], peer(z + 1, p))

    def down_copy(ph, s):
        block = xg.at[ph, s]
        return remote(block, block, down_ss.at[ph, s], line_rs.at[ph, s], peer(z - 1, p))

    def row_copy(ph, s, q):
        return remote(
            send_rows.at[ph, s, q], recv_rows.at[ph, s, p], y_ss.at[ph, s, q],
            y_rs.at[ph, s, p], peer(z, q),
        )

    def row_wait(ph, s, q):
        remote(
            send_rows.at[ph, s, q], recv_rows.at[ph, s, q], y_ss.at[ph, s, q],
            y_rs.at[ph, s, q], peer(z, q),
        ).wait_recv()

    def ret_copy(ph, s, q):
        return remote(
            recv_rows.at[ph, s, q], ret_rows.at[ph, s, p], r_ss.at[ph, s, q],
            r_rs.at[ph, s, p], peer(z, q),
        )

    def ret_wait(ph, s, q):
        remote(
            recv_rows.at[ph, s, q], ret_rows.at[ph, s, q], r_ss.at[ph, s, q],
            r_rs.at[ph, s, q], peer(z, q),
        ).wait_recv()

    mate = z + 1 - 2 * (z % 2)
    inner = (z >= 1) & (z <= LAYERS - 2)
    outer = (z < 1) | (z > LAYERS - 2)
    other_inner = 2 - z // 2

    def part_copy(ph, s):
        return remote(
            part.at[ph, s], zrecv.at[ph, z], p_ss.at[ph, s], p_rs.at[ph, z], peer(s, p)
        )

    def part_wait(ph, s):
        remote(
            part.at[ph, s], zrecv.at[ph, s], p_ss.at[ph, s], p_rs.at[ph, s], peer(s, p)
        ).wait_recv()

    def chain_copy(ph, s):
        return remote(
            part.at[ph, s], chain.at[ph], p_ss.at[ph, s], chain_rs.at[ph], peer(other_inner, p)
        )

    def relay_copy(ph, s):
        return remote(
            part.at[ph, s], relay.at[ph, s % 2], p_ss.at[ph, s], relay_rs.at[ph, s % 2],
            peer(mate, p),
        )

    def dot_copy(s):
        return remote(dsend.at[s], drecv.at[z], d_ss.at[s], d_rs.at[z], peer(s, p))

    def forward(ph, s):
        @pl.when((s <= z) & (z < LAYERS - 1))
        def _():
            up_copy(ph, s).start()

        @pl.when((s >= z) & (z > 0))
        def _():
            down_copy(ph, s).start()

    own_copies[0].wait()
    forward(0, z)
    for o in range(1, LAYERS):
        meta_copy(o).start()
    for copy in w_copies:
        copy.start()
    own_copies[1].wait()

    row_id = lax.broadcasted_iota(jnp.int32, (cap, tok_rows), 0).astype(jnp.float32)

    def picks(s):
        tables = meta[s, z]
        return [tables[q : q + 1] == row_id for q in range(PLANE)], tables

    def line_stage(i):
        ph, t = item(i)
        s = order(t)

        @pl.when(t > 0)
        def _():
            @pl.when(ph == 0)
            def _():
                meta_wait(s)

            remote(
                xg.at[ph, s], xg.at[ph, s], up_ss.at[ph, s], line_rs.at[ph, s], peer(s, p)
            ).wait_recv()
            forward(ph, s)

    def send_stage(i):
        ph, t = item(i)
        s = order(t)

        hits, _ = picks(s)
        select = jnp.concatenate(
            [jnp.where(hit, 1.0, 0.0) for hit in hits], axis=0
        ).astype(jnp.bfloat16)
        rows = jnp.dot(select, xg[ph, s], preferred_element_type=jnp.float32)
        send_rows[ph, s] = rows.astype(jnp.bfloat16).reshape(PLANE, cap, width)
        for o in range(1, PLANE):
            row_copy(ph, s, (p + o) % PLANE).start()
        recv_rows[ph, s, p] = send_rows[ph, s, p]

    def expert_stage(i):
        ph, t = item(i)
        s = order(t)
        for o in range(1, PLANE):
            row_wait(ph, s, (p + o) % PLANE)

        @pl.when(ph == 0)
        def _():
            rows = recv_rows[0, s].reshape(slots, width)
            gate = jnp.dot(rows, wg[...], preferred_element_type=jnp.float32)
            upper = jnp.dot(rows, wu[...], preferred_element_type=jnp.float32)
            gate_buf[s] = gate
            up_buf[s] = upper
            hidden = (gate * jax.nn.sigmoid(gate) * upper).astype(jnp.bfloat16)
            out = jnp.dot(hidden, wd[...], preferred_element_type=jnp.float32)
            recv_rows[0, s] = out.astype(jnp.bfloat16).reshape(PLANE, cap, width)

        @pl.when(ph == 1)
        def _():
            rows = recv_rows[1, s].reshape(slots, width)
            d_hidden = nt_dot(rows, wd[...])
            gate = gate_buf[s]
            upper = up_buf[s]
            sig = jax.nn.sigmoid(gate)
            d_gate = (d_hidden * upper * sig * (1.0 + gate * (1.0 - sig))).astype(jnp.bfloat16)
            d_upper = (d_hidden * (gate * sig)).astype(jnp.bfloat16)
            back = nt_dot(d_gate, wg[...]) + nt_dot(d_upper, wu[...])
            recv_rows[1, s] = back.astype(jnp.bfloat16).reshape(PLANE, cap, width)

        for o in range(1, PLANE):
            ret_copy(ph, s, (p + o) % PLANE).start()
        ret_rows[ph, s, p] = recv_rows[ph, s, p]

    def combine_stage(i):
        ph, t = item(i)
        s = order(t)
        for o in range(1, PLANE):
            ret_wait(ph, s, (p + o) % PLANE)
        hits, tables = picks(s)
        weights = jnp.concatenate(
            [
                jnp.where(hits[q], tables[PLANE + q : PLANE + q + 1], 0.0)
                for q in range(PLANE)
            ],
            axis=0,
        )
        high = weights.astype(jnp.bfloat16)
        low = (weights - high.astype(jnp.float32)).astype(jnp.bfloat16)
        rows = ret_rows[ph, s].reshape(slots, width)
        first = (((0,), (0,)), ((), ()))
        total = lax.dot_general(high, rows, first, preferred_element_type=jnp.float32)
        total = total + lax.dot_general(low, rows, first, preferred_element_type=jnp.float32)
        total = total.astype(jnp.bfloat16)

        @pl.when(t == 0)
        def _():
            zrecv[ph, z] = total

        @pl.when(t > 0)
        def _():
            part[ph, s] = total

        @pl.when((t == 1) & (outer | (ph >= CHAINED)))
        def _():
            part_copy(ph, s).start()

        @pl.when((t > 1) & outer)
        def _():
            relay_copy(ph, s).start()

        @pl.when(ph == 1)
        def _():
            out = ret_rows[0, s].reshape(slots, width)
            pairs = nt_dot(out, xg[1, s])
            sums = [
                jnp.sum(
                    jnp.where(hits[q], pairs[q * cap : (q + 1) * cap], 0.0), axis=0, keepdims=True
                )
                for q in range(PLANE)
            ]
            table = jnp.concatenate(sums + [jnp.zeros((8 - PLANE, tok_rows), jnp.float32)], axis=0)

            @pl.when(t == 0)
            def _():
                drecv[z] = table

            @pl.when(t > 0)
            def _():
                dsend[s] = table
                dot_copy(s).start()

    def relay_stage(i):
        ph, t = item(i)
        s = order(t)

        @pl.when((t > 1) & inner)
        def _():
            relay_copy(ph, s).wait_recv()
            total = part[ph, s].astype(jnp.float32) + relay[ph, s % 2].astype(jnp.float32)
            part[ph, s] = total.astype(jnp.bfloat16)

            @pl.when((t < LAYERS - 1) | (ph >= CHAINED))
            def _():
                part_copy(ph, s).start()

            @pl.when((t == LAYERS - 1) & (ph < CHAINED))
            def _():
                chain_copy(ph, s).start()

    def chain_stage(i):
        ph, t = item(i)

        @pl.when((t == LAYERS - 1) & (ph < CHAINED) & inner)
        def _():
            chain_copy(ph, mate).wait_recv()
            total = part[ph, mate].astype(jnp.float32) + chain[ph].astype(jnp.float32)
            part[ph, mate] = total.astype(jnp.bfloat16)
            part_copy(ph, mate).start()

    items = 2 * LAYERS

    def grad_stage(i):
        @pl.when(i == 0)
        def _():
            forward(1, z)

    def weight_stage(i):
        @pl.when(i == 0)
        def _():
            for copy in w_copies:
                copy.wait()

    stages = {
        "line": line_stage,
        "grad": grad_stage,
        "send": send_stage,
        "weight": weight_stage,
        "expert": expert_stage,
        "combine": combine_stage,
        "relay": relay_stage,
        "chain": chain_stage,
    }
    last = items + max(lag for _, lag in SCHEDULE)

    def step(i, carry):
        for name, lag in SCHEDULE:
            pl.when((i >= lag) & (i < items + lag))(functools.partial(stages[name], i - lag))
        return carry

    lax.fori_loop(0, last, step, 0)

    for ph, target in ((0, mixed_ref), (1, grad_ref)):
        part_wait(ph, mate)
        total = zrecv[ph, z].astype(jnp.float32) + zrecv[ph, mate].astype(jnp.float32)

        def add_other(target=target, ph=ph, total=total):
            part_wait(ph, other_inner)
            wide = total + zrecv[ph, other_inner].astype(jnp.float32)
            target[...] = wide.astype(jnp.bfloat16)

        if ph < CHAINED:

            @pl.when(outer)
            def _():
                target[...] = total.astype(jnp.bfloat16)

            pl.when(inner)(add_other)
        else:
            add_other()
    for o in range(1, LAYERS):
        s = (z + o) % LAYERS
        remote(dsend.at[s], drecv.at[s], d_ss.at[s], d_rs.at[s], peer(s, p)).wait_recv()
    table = jnp.concatenate([drecv[layer, :PLANE] for layer in range(LAYERS)], axis=0)
    for k in range(fanout):
        hit = ids_ref[k : k + 1, :] == experts
        gcomb_ref[k : k + 1, :] = jnp.sum(jnp.where(hit, table, 0.0), axis=0, keepdims=True)

    for o in range(1, LAYERS):
        s = (z + o) % LAYERS
        meta_copy(o).wait_send()
        dot_copy(s).wait_send()
        for ph in range(2):
            part_copy(ph, s).wait_send()

    def drain(i, carry):
        ph, s = i // LAYERS, i % LAYERS

        @pl.when((s <= z) & (z < LAYERS - 1))
        def _():
            up_copy(ph, s).wait_send()

        @pl.when((s >= z) & (z > 0))
        def _():
            down_copy(ph, s).wait_send()

        for o in range(1, PLANE):
            row_copy(ph, s, (p + o) % PLANE).wait_send()
            ret_copy(ph, s, (p + o) % PLANE).wait_send()
        return carry

    lax.fori_loop(0, items, drain, 0)


def fused_on_device(tokens, cotangent, expert_ids, combine, w_gate, w_up, w_down):
    holders = lax.axis_size("expert")
    tok_rows, width = tokens.shape
    fanout = expert_ids.shape[1]
    cap = 2 * tok_rows * fanout // holders
    inner = w_gate.shape[2]
    slots = PLANE * cap
    bf, f32 = jnp.bfloat16, jnp.float32
    hbm = pl.BlockSpec(memory_space=pl.ANY)
    vmem = pl.BlockSpec(memory_space=pltpu.VMEM)
    dma = pltpu.SemaphoreType.DMA
    rows = pltpu.VMEM((2, LAYERS, PLANE, cap, width), bf)
    blocks = pltpu.VMEM((2, LAYERS, tok_rows, width), bf)
    mixed, grad_tokens, gcomb = pl.pallas_call(
        fused_kernel,
        out_shape=(
            jax.ShapeDtypeStruct((tok_rows, width), bf),
            jax.ShapeDtypeStruct((tok_rows, width), bf),
            jax.ShapeDtypeStruct((fanout, tok_rows), f32),
        ),
        in_specs=[hbm, hbm, vmem, vmem, hbm, hbm, hbm],
        out_specs=(vmem, vmem, vmem),
        scratch_shapes=[
            pltpu.VMEM(w_gate.shape[1:], bf),
            pltpu.VMEM(w_up.shape[1:], bf),
            pltpu.VMEM(w_down.shape[1:], bf),
            blocks,
            pltpu.VMEM((LAYERS, LAYERS, 2 * PLANE, tok_rows), f32),
            rows,
            rows,
            pltpu.VMEM((LAYERS, slots, inner), f32),
            pltpu.VMEM((LAYERS, slots, inner), f32),
            rows,
            blocks,
            blocks,
            pltpu.VMEM((2, 2, tok_rows, width), bf),
            pltpu.VMEM((2, tok_rows, width), bf),
            pltpu.VMEM((LAYERS, 8, tok_rows), f32),
            pltpu.VMEM((LAYERS, 8, tok_rows), f32),
            dma((3,)),
            dma((2,)),
            dma((LAYERS,)),
            dma((LAYERS,)),
            dma((2, LAYERS)),
            dma((2, LAYERS)),
            dma((2, LAYERS)),
            dma((2, LAYERS, PLANE)),
            dma((2, LAYERS, PLANE)),
            dma((2, LAYERS, PLANE)),
            dma((2, LAYERS, PLANE)),
            dma((2, LAYERS)),
            dma((2, LAYERS)),
            dma((LAYERS,)),
            dma((LAYERS,)),
            dma((2, 2)),
            dma((2,)),
        ],
        compiler_params=pltpu.CompilerParams(
            collective_id=0, has_side_effects=True, vmem_limit_bytes=60 * 2**20
        ),
    )(tokens, cotangent, expert_ids.T, combine.T, w_gate, w_up, w_down)
    return mixed, grad_tokens, gcomb.T


def solution(mesh):
    placed = (
        P(("groups", "expert"), None),
        P(("groups", "expert"), None),
        P(("groups", "expert"), None),
        P(("groups", "expert"), None),
        P("expert", None, None),
        P("expert", None, None),
        P("expert", None, None),
    )
    fits = mesh.shape["expert"] == PLANE * LAYERS
    return jax.shard_map(
        fused_on_device if fits else on_device,
        mesh=mesh,
        in_specs=placed,
        out_specs=(
            P(("groups", "expert"), None),
            P(("groups", "expert"), None),
            P(("groups", "expert"), None),
        ),
        check_vma=False,
    )
```
